32 devices in a mesh: tm: 4 (over z), space: 8 (over y, x, core).
Axes of the slice: x: 2, y: 2, z: 4, core: 2. Of those that a mesh axis runs over, the one named last changes fastest.
Arguments:
- noise_field: float32 [8, 4, 8, 6, 256], P(None, 'tm', 'space'), may hold values from -6 to 6
- gauge_links: float32 [4, 3, 4, 8, 6, 256], P(None, None, 'tm', 'space'), may hold values from -2.5 to 2.5
- clover: float32 [2, 6, 4, 8, 12, 256], P(None, None, 'tm', 'space'), may hold values from -0.9 to 0.9
- eigvecs: float32 [48, 4, 8, 6, 256], P(None, 'tm', 'space'), may hold values from -0.0546875 to 0.0546875
- partner: int32 [48], replicated, may hold values from 0 to 47, each once
- dilution: int32 [8], replicated, may hold values from 0 to 3
- boundary: int32 [4], replicated, may hold values from 0 to 1
Outputs:
- perambulator: float32 [32, 4, 96], P('space', 'tm')
- correlator: float32 [32, 4, 4], P('space', 'tm')
The draws below stay inside these ranges and needn't reach their ends.
Inputs may be any that keep to these rules, and one draw needn't show every extreme that they name: `partner`: each of 0 to 47 once.
All inputs are finite; a program needn't handle non-finite values.
Results may differ from the reference program's by a relative error of at most 0.00029.
Values sent between devices are 32-bit elements; how exact they have to be, the bound alone decides.
A program may use at most 64 MiB of HBM per device.

```python
import jax
import jax.numpy as jnp
from jax import lax

NEV = 48
NSRC = 8
ITERS = 4
DILUTE = 4
SIDE = 16
LZ = 1
NT = 4
NZ = 8
N_SPACE = 8


def with_ends(entries, stream_key, low, high):
    shape = entries.shape
    index_at = [jax.random.randint(jax.random.fold_in(stream_key, axis), (), 0, shape[axis]) for axis in range(len(shape))]
    entries = entries.at[tuple(index_at)].set(low)
    longest = shape.index(max(shape))
    index_at[longest] = (index_at[longest] + 1) % shape[longest]
    return entries.at[tuple(index_at)].set(high)


def levels(stream_key, shape, cuts, least, top_value):
    def one(dim, shards_of):
        draws = jax.random.uniform(jax.random.fold_in(jax.random.fold_in(stream_key, 6), dim), (shards_of,), jnp.float32, least / len(cuts), top_value / len(cuts))
        return jnp.repeat(jnp.exp(draws), shape[dim] // shards_of).reshape((-1,) + (1,) * (len(shape) - dim - 1))

    gain = one(*cuts[0])
    for cut in cuts[1:]:
        gain = gain * one(*cut)
    return gain


def bell_draw(rng, shape, width, most, cuts=(), kind=jnp.bfloat16):
    values = width * jax.random.normal(rng, shape, jnp.float32)
    if cuts:
        values = values * levels(rng, shape, cuts, -0.22, 0.18)
    return jnp.clip(values, -most, most).astype(kind)


def setup_inputs(seed: int = 0) -> dict:
    key_list = jax.random.split(jax.random.key(seed), 8)
    noise_field = bell_draw(key_list[0], (NSRC, NT, NZ, 6, SIDE * SIDE), 1.0, 6.0, ((1, 4), (2, 8)), jnp.float32)
    gauge_links = bell_draw(key_list[1], (4, 3, NT, NZ, 6, SIDE * SIDE), 6 ** -0.5, 2.5, ((2, 4), (3, 8)), jnp.float32)
    clover = bell_draw(key_list[2], (2, 6, NT, NZ, 12, SIDE * SIDE), 0.15, 0.9, ((2, 4), (3, 8)), jnp.float32)
    eigvecs = bell_draw(key_list[3], (NEV, NT, NZ, 6, SIDE * SIDE), (6 * SIDE * SIDE * LZ * N_SPACE) ** -0.5, 0.0546875, ((1, 4), (2, 8)), jnp.float32)
    partner = jax.random.permutation(key_list[4], NEV).astype(jnp.int32)
    dilution = with_ends(jax.random.randint(key_list[5], (NSRC,), 0, DILUTE), jax.random.fold_in(key_list[5], 1), 0, DILUTE - 1).astype(jnp.int32)
    boundary = with_ends(jax.random.randint(key_list[6], (4,), 0, 2), jax.random.fold_in(key_list[6], 1), 0, 1).astype(jnp.int32)
    return {"noise_field": noise_field, "gauge_links": gauge_links, "clover": clover, "eigvecs": eigvecs, "partner": partner, "dilution": dilution, "boundary": boundary}


diag_term = 4.1
step_size = 0.2
twist_table = (
    (((1, 0, -1), (0, 0, -1)), ((1, 0, 1), (0, 0, 1))),
    (((1, -1, 0), (0, 1, 0)), ((1, 1, 0), (0, -1, 0))),
    (((0, 0, -1), (1, 0, 1)), ((0, 0, 1), (1, 0, -1))),
    (((0, 1, 0), (1, 1, 0)), ((0, 1, 0), (1, 1, 0))),
)


def pair_add(first_pair, second_pair):
    return (first_pair[0] + second_pair[0], first_pair[1] + second_pair[1])


def pair_sub(first_pair, second_pair):
    return (first_pair[0] - second_pair[0], first_pair[1] - second_pair[1])


def pair_scale(factor, value_pair):
    return (factor * value_pair[0], factor * value_pair[1])


def scaled(value_pair, real_coef, imag_coef):
    if imag_coef == 0:
        return (real_coef * value_pair[0], real_coef * value_pair[1])
    return (-imag_coef * value_pair[1], imag_coef * value_pair[0])


def spin_twist(direction, adjoint, half_pair):
    outputs = []
    for source_spin, real_coef, imag_coef in twist_table[direction][adjoint]:
        picked = (half_pair[0][:, source_spin], half_pair[1][:, source_spin])
        outputs.append(scaled(picked, real_coef, imag_coef))
    return (jnp.stack([outputs[0][0], outputs[1][0]], 1), jnp.stack([outputs[0][1], outputs[1][1]], 1))


def split_spins(spinor_pair):
    upper_half = (spinor_pair[0][:, 0:2], spinor_pair[1][:, 0:2])
    lower_half = (spinor_pair[0][:, 2:4], spinor_pair[1][:, 2:4])
    return upper_half, lower_half


def link_apply(link_real, link_imag, half_pair):
    total_real = 0.0
    total_imag = 0.0
    for column in range(3):
        matrix_real = jnp.moveaxis(link_real[:, :, :, column, :], 0, 2)
        matrix_imag = jnp.moveaxis(link_imag[:, :, :, column, :], 0, 2)
        vector_real = half_pair[0][..., column:column + 1, :]
        vector_imag = half_pair[1][..., column:column + 1, :]
        total_real = total_real + matrix_real * vector_real - matrix_imag * vector_imag
        total_imag = total_imag + matrix_real * vector_imag + matrix_imag * vector_real
    return (total_real, total_imag)


def link_adjoint(link_real, link_imag, half_pair):
    total_real = 0.0
    total_imag = 0.0
    for matrix_row in range(3):
        matrix_real = link_real[matrix_row]
        matrix_imag = link_imag[matrix_row]
        vector_real = half_pair[0][..., matrix_row:matrix_row + 1, :]
        vector_imag = half_pair[1][..., matrix_row:matrix_row + 1, :]
        total_real = total_real + matrix_real * vector_real + matrix_imag * vector_imag
        total_imag = total_imag + matrix_real * vector_imag - matrix_imag * vector_real
    return (total_real, total_imag)


def plane_shift(values, direction, forward, edge_sign):
    flat_index = lax.broadcasted_iota(jnp.int32, values.shape, values.ndim - 1)
    if direction == 0:
        coordinate = flat_index % SIDE
        if forward:
            return jnp.where(coordinate == SIDE - 1, edge_sign * jnp.roll(values, SIDE - 1, axis=-1), jnp.roll(values, -1, axis=-1))
        return jnp.where(coordinate == 0, edge_sign * jnp.roll(values, 1 - SIDE, axis=-1), jnp.roll(values, 1, axis=-1))
    coordinate = flat_index // SIDE
    if forward:
        rolled = jnp.roll(values, -SIDE, axis=-1)
        return jnp.where(coordinate == SIDE - 1, edge_sign * rolled, rolled)
    rolled = jnp.roll(values, SIDE, axis=-1)
    return jnp.where(coordinate == 0, edge_sign * rolled, rolled)


def lattice_shift(values, axis_dim, forward, edge_sign):
    extent = values.shape[axis_dim]
    position = lax.broadcasted_iota(jnp.int32, values.shape, axis_dim)
    if forward:
        rolled = jnp.roll(values, -1, axis=axis_dim)
        return jnp.where(position == extent - 1, edge_sign * rolled, rolled)
    rolled = jnp.roll(values, 1, axis=axis_dim)
    return jnp.where(position == 0, edge_sign * rolled, rolled)


def clover_apply(clover, spinor_pair):
    parts_real = []
    parts_imag = []
    for chiral in range(2):
        block_real = clover[chiral][:, :, :, 0::2, :]
        block_imag = clover[chiral][:, :, :, 1::2, :]
        total_real = 0.0
        total_imag = 0.0
        for column in range(6):
            spin_index = 2 * chiral + column // 3
            color_index = column % 3
            vector_real = spinor_pair[0][:, spin_index, :, :, color_index, :][:, None]
            vector_imag = spinor_pair[1][:, spin_index, :, :, color_index, :][:, None]
            entry_real = block_real[:, :, :, column, :]
            entry_imag = block_imag[:, :, :, column, :]
            total_real = total_real + entry_real * vector_real - entry_imag * vector_imag
            total_imag = total_imag + entry_real * vector_imag + entry_imag * vector_real
        counts = total_real.shape
        new_shape = (counts[0], 2, 3) + counts[2:]
        parts_real.append(total_real.reshape(new_shape).transpose(0, 1, 3, 4, 2, 5))
        parts_imag.append(total_imag.reshape(new_shape).transpose(0, 1, 3, 4, 2, 5))
    return (jnp.concatenate(parts_real, 1), jnp.concatenate(parts_imag, 1))


def recombine(direction, ahead_linked, behind_moved):
    top_part = pair_add(ahead_linked, behind_moved)
    bottom_part = pair_sub(spin_twist(direction, 1, behind_moved), spin_twist(direction, 1, ahead_linked))
    return (jnp.concatenate([top_part[0], bottom_part[0]], 1), jnp.concatenate([top_part[1], bottom_part[1]], 1))


def pair_map(function_one, value_pair):
    return (function_one(value_pair[0]), function_one(value_pair[1]))


def apply_operator(spinor_pair, gauge_links, clover, phase_signs):
    upper_half, lower_half = split_spins(spinor_pair)
    hopping = (0.0, 0.0)
    for direction in range(4):
        link_real = gauge_links[direction][:, :, :, 0::2, :]
        link_imag = gauge_links[direction][:, :, :, 1::2, :]
        twisted = spin_twist(direction, 0, lower_half)
        ahead_half = pair_sub(upper_half, twisted)
        behind_half = link_adjoint(link_real, link_imag, pair_add(upper_half, twisted))
        edge_sign = phase_signs[direction]
        if direction < 2:
            ahead_moved = pair_map(lambda values: plane_shift(values, direction, True, edge_sign), ahead_half)
            behind_moved = pair_map(lambda values: plane_shift(values, direction, False, edge_sign), behind_half)
        else:
            axis_dim = 3 if direction == 2 else 2
            ahead_moved = pair_map(lambda values: lattice_shift(values, axis_dim, True, edge_sign), ahead_half)
            behind_moved = pair_map(lambda values: lattice_shift(values, axis_dim, False, edge_sign), behind_half)
        ahead_linked = link_apply(link_real, link_imag, ahead_moved)
        hopping = pair_add(hopping, recombine(direction, ahead_linked, behind_moved))
    clovered = clover_apply(clover, spinor_pair)
    result = pair_add(pair_scale(diag_term, spinor_pair), clovered)
    return pair_sub(result, pair_scale(0.5, hopping))


def build_source(noise_field, dilution, time_index):
    sources = noise_field.shape[0]
    spin_mask = (lax.broadcasted_iota(jnp.int32, (sources, 4), 1) == lax.broadcasted_iota(jnp.int32, (sources, 4), 0) % 4).astype(jnp.float32)
    time_mask = (time_index[None, :] % DILUTE == dilution[:, None]).astype(jnp.float32)
    source_weight = spin_mask[:, :, None, None, None, None] * time_mask[:, None, :, None, None, None]
    return (source_weight * noise_field[:, None, :, :, 0::2, :], source_weight * noise_field[:, None, :, :, 1::2, :])


def project(solution, eigvecs):
    counts = solution[0].shape
    flat_shape = (counts[0] * counts[1], counts[2], counts[3] * counts[4] * counts[5])
    solve_result_real = solution[0].reshape(flat_shape)
    solve_result_imag = solution[1].reshape(flat_shape)
    eig_shape = (eigvecs.shape[0], eigvecs.shape[1], flat_shape[2])
    eigenmode_real = eigvecs[:, :, :, 0::2, :].reshape(eig_shape)
    eigenmode_imag = eigvecs[:, :, :, 1::2, :].reshape(eig_shape)
    highest_value = lax.Precision.HIGHEST
    real_component = jnp.einsum("gdc,xdc->xdg", eigenmode_real, solve_result_real, precision=highest_value) + jnp.einsum("gdc,xdc->xdg", eigenmode_imag, solve_result_imag, precision=highest_value)
    imaginary_component = jnp.einsum("gdc,xdc->xdg", eigenmode_real, solve_result_imag, precision=highest_value) - jnp.einsum("gdc,xdc->xdg", eigenmode_imag, solve_result_real, precision=highest_value)
    return jnp.concatenate([real_component, imaginary_component], 2)


def weigh_pairs(peram_block, partner):
    vectors = partner.shape[0]
    onehot = (partner[:, None] == lax.broadcasted_iota(jnp.int32, (vectors, vectors), 1)).astype(jnp.float32)
    highest_value = lax.Precision.HIGHEST
    real_component = jnp.einsum("jtk,kl->jtl", peram_block[:, :, :vectors], onehot, precision=highest_value)
    imaginary_component = jnp.einsum("jtk,kl->jtl", peram_block[:, :, vectors:], onehot, precision=highest_value)
    return jnp.concatenate([real_component, imaginary_component], 2)


def reference(noise_field, gauge_links, clover, eigvecs, partner, dilution, boundary):
    phase_signs = 1.0 - 2.0 * boundary.astype(jnp.float32)
    time_index = jnp.arange(NT, dtype=jnp.int32)
    source = build_source(noise_field, dilution, time_index)
    solution = pair_scale(step_size, source)
    for iteration in range(ITERS):
        applied = apply_operator(solution, gauge_links, clover, phase_signs)
        solution = pair_add(solution, pair_scale(step_size, pair_sub(source, applied)))
    perambulator = project(solution, eigvecs)
    weighted = weigh_pairs(perambulator, partner)
    correlator = jnp.einsum("jac,jbc->jab", weighted, perambulator, precision=lax.Precision.HIGHEST)
    return perambulator, correlator
```

```python
import functools
import math

import jax
import jax.numpy as jnp
from jax import lax
from jax.experimental import pallas as pl
from jax.experimental.pallas import tpu as pltpu
from jax.sharding import PartitionSpec as P

ITERS = 4
DILUTE = 4
MESH = pl.DeviceIdType.MESH

diag_term = 4.1
step_size = 0.2
twist_table = (
    (((1, 0, -1), (0, 0, -1)), ((1, 0, 1), (0, 0, 1))),
    (((1, -1, 0), (0, 1, 0)), ((1, 1, 0), (0, -1, 0))),
    (((0, 0, -1), (1, 0, 1)), ((0, 0, 1), (1, 0, -1))),
    (((0, 1, 0), (1, 1, 0)), ((0, 1, 0), (1, 1, 0))),
)


def signed_add(total, sign, value):
    return total + value if sign > 0 else total - value


def twist_terms(real_coef, imag_coef, real, imag):
    if imag_coef == 0:
        return (real_coef, real), (real_coef, imag)
    return (-imag_coef, imag), (imag_coef, real)


def kernel(
    times, planes, noise, gauge, clover, eigvecs, partner, dilution, boundary,
    per_out, cor_out,
    links, clov, src, sol, acc, sbuf, rbuf, eig_hi, eig_lo, part, red, own, gat, onehot,
    ssem, rsem, red_ssem, red_rsem, gat_ssem, gat_rsem,
):
    t_me = lax.axis_index("tm")
    z_me = lax.axis_index("space")
    t_up, t_down = lax.rem(t_me + 1, times), lax.rem(t_me + times - 1, times)
    z_up, z_down = lax.rem(z_me + 1, planes), lax.rem(z_me + planes - 1, planes)

    barrier = pltpu.get_barrier_semaphore()
    for off in range(1, times):
        pl.semaphore_signal(
            barrier, inc=1, device_id={"tm": lax.rem(t_me + off, times)}, device_id_type=MESH
        )
    for off in range(1, planes):
        pl.semaphore_signal(
            barrier, inc=1, device_id={"space": lax.rem(z_me + off, planes)}, device_id_type=MESH
        )

    nsrc, sites = noise.shape[0], noise.shape[-1]
    side = math.isqrt(sites)
    nev = eigvecs.shape[0]
    row = (1, sites)
    lane = lax.broadcasted_iota(jnp.int32, row, 1)
    x_row, y_row = lax.rem(lane, side), lax.div(lane, side)
    phases = [1.0 - 2.0 * boundary[mu].astype(jnp.float32) for mu in range(4)]
    half_step = 0.5 * step_size
    one = jnp.ones(row, jnp.float32)
    signs = (
        jnp.where(x_row == side - 1, phases[0], one) * half_step,
        jnp.where(y_row == side - 1, phases[1], one) * half_step,
        jnp.where(z_me == planes - 1, phases[2], 1.0) * half_step * one,
        jnp.where(t_me == times - 1, phases[3], 1.0) * half_step * one,
    )
    for mu in range(4):
        for col in range(3):
            for p in range(2):
                k = 2 * col + p
                value = gauge[mu, :, 0, 0, k : k + 1, :] * signs[mu][None]
                links[mu, p, :, col] = jnp.broadcast_to(value, (3, nsrc, sites))

    field = (nsrc, sites)
    source_row = lax.broadcasted_iota(jnp.int32, field, 0)
    spin_row = lax.rem(source_row, 4)
    t_mod = lax.rem(t_me, DILUTE)
    weight = jnp.zeros(field, jnp.float32)
    for j in range(nsrc):
        chosen = jnp.where(dilution[j] == t_mod, step_size, 0.0)
        weight = jnp.where(source_row == j, chosen, weight)
    for color in range(3):
        for p in range(2):
            value = noise[:, 0, 0, 2 * color + p, :] * weight
            for s in range(4):
                src[p, s, color] = jnp.where(spin_row == s, value, 0.0)
    sol[...] = src[...]

    for b in range(6):
        for p in range(2):
            k = 2 * b + p
            value = clover[:, :, 0, 0, k : k + 1, :] * (-step_size)
            clov[:, p, :, b] = jnp.broadcast_to(value, (2, 6, nsrc, sites))

    for color in range(3):
        real = eigvecs[:, 0, 0, 2 * color, :]
        imag = eigvecs[:, 0, 0, 2 * color + 1, :]
        for p, (top, bottom) in enumerate(((real, -imag), (imag, real))):
            lo = (2 * color + p) * sites
            whole = jnp.concatenate([top, bottom], 0)
            high = whole.astype(jnp.bfloat16)
            eig_hi[:, lo : lo + sites] = high
            eig_lo[:, lo : lo + sites] = (whole - high.astype(jnp.float32)).astype(jnp.bfloat16)

    out_lane = lax.broadcasted_iota(jnp.int32, (1, onehot.shape[1]), 1)
    for k in range(nev):
        for p in range(2):
            onehot[p * nev + k : p * nev + k + 1, :] = jnp.where(
                out_lane == partner[k] + p * nev, 1.0, 0.0
            )

    def half(mu, sign):
        real, imag = [], []
        for h in range(2):
            pick, rc, ic = twist_table[mu][0][h]
            tr, ti = twist_terms(rc, ic, sol[0, 2 + pick], sol[1, 2 + pick])
            real.append(signed_add(sol[0, h], sign * tr[0], tr[1]))
            imag.append(signed_add(sol[1, h], sign * ti[0], ti[1]))
        return jnp.stack(real), jnp.stack(imag)

    def forward(mu, vr, vi):
        real = imag = None
        for c in range(3):
            ur, ui = links[mu, 0, :, c][None], links[mu, 1, :, c][None]
            ar, ai = vr[:, c : c + 1], vi[:, c : c + 1]
            dr, di = ur * ar - ui * ai, ur * ai + ui * ar
            real, imag = (dr, di) if c == 0 else (real + dr, imag + di)
        return real, imag

    def adjoint(mu, vr, vi):
        real = imag = None
        for c in range(3):
            ur, ui = links[mu, 0, c][None], links[mu, 1, c][None]
            ar, ai = vr[:, c : c + 1], vi[:, c : c + 1]
            dr, di = ur * ar + ui * ai, ur * ai - ui * ar
            real, imag = (dr, di) if c == 0 else (real + dr, imag + di)
        return real, imag

    def gather_in(mu, ahead, behind):
        diff = (behind[0] - ahead[0], behind[1] - ahead[1])
        for p in range(2):
            acc[p, 0:2] += ahead[p] + behind[p]
        for h in range(2):
            pick, rc, ic = twist_table[mu][1][h]
            terms = twist_terms(rc, ic, diff[0][pick], diff[1][pick])
            for p in range(2):
                acc[p, 2 + h] = signed_add(acc[p, 2 + h], terms[p][0], terms[p][1])

    flat = (6 * nsrc, sites)
    flat_x = lax.rem(lax.broadcasted_iota(jnp.int32, flat, 1), side)

    def shift(mu, ahead, value):
        value = value.reshape(flat)
        if mu == 0:
            if ahead:
                moved = jnp.where(
                    flat_x == side - 1,
                    pltpu.roll(value, side - 1, 1),
                    pltpu.roll(value, sites - 1, 1),
                )
            else:
                moved = jnp.where(
                    flat_x == 0,
                    pltpu.roll(value, sites - side + 1, 1),
                    pltpu.roll(value, 1, 1),
                )
        else:
            moved = pltpu.roll(value, sites - side if ahead else side, 1)
        return moved.reshape(2, 3, nsrc, sites)

    targets = ({"tm": t_down}, {"tm": t_up}, {"space": z_down}, {"space": z_up})

    def copy(it, d):
        return pltpu.make_async_remote_copy(
            src_ref=sbuf.at[it, d],
            dst_ref=rbuf.at[it, d],
            send_sem=ssem.at[it, d],
            recv_sem=rsem.at[it, d],
            device_id=targets[d],
            device_id_type=MESH,
        )

    pl.semaphore_wait(barrier, times + planes - 2)

    def iteration(it, carry):
        for mu, d in ((3, 0), (2, 2)):
            ahead = half(mu, -1)
            sbuf[it, d, 0], sbuf[it, d, 1] = ahead
            copy(it, d).start()
            behind = adjoint(mu, *half(mu, 1))
            sbuf[it, d + 1, 0], sbuf[it, d + 1, 1] = behind
            copy(it, d + 1).start()
        keep = 1.0 - step_size * diag_term
        for h in range(2):
            real = imag = None
            for b in range(6):
                cr, ci = clov[h, 0, :, b], clov[h, 1, :, b]
                vr = sol[0, 2 * h + b // 3, b % 3][None]
                vi = sol[1, 2 * h + b // 3, b % 3][None]
                dr, di = cr * vr - ci * vi, cr * vi + ci * vr
                real, imag = (dr, di) if b == 0 else (real + dr, imag + di)
            for p, value in enumerate((real, imag)):
                lo = 2 * h
                acc[p, lo : lo + 2] = (
                    value.reshape(2, 3, nsrc, sites)
                    + keep * sol[p, lo : lo + 2]
                    + src[p, lo : lo + 2]
                )
        for mu in range(2):
            ahead = half(mu, -1)
            ahead = forward(mu, shift(mu, True, ahead[0]), shift(mu, True, ahead[1]))
            behind = adjoint(mu, *half(mu, 1))
            behind = (shift(mu, False, behind[0]), shift(mu, False, behind[1]))
            gather_in(mu, ahead, behind)
        for mu, d in ((2, 2), (3, 0)):
            copy(it, d).wait()
            copy(it, d + 1).wait()
            ahead = forward(mu, rbuf[it, d, 0], rbuf[it, d, 1])
            gather_in(mu, ahead, (rbuf[it, d + 1, 0], rbuf[it, d + 1, 1]))
        sol[...] = acc[...]
        return carry

    lax.fori_loop(0, ITERS, iteration, 0)

    pieces = []
    for color in range(3):
        for p in range(2):
            pieces.append(sol[p, :, color].reshape(4 * nsrc, sites))
    whole = jnp.concatenate(pieces, 1)
    high = whole.astype(jnp.bfloat16)
    low = (whole - high.astype(jnp.float32)).astype(jnp.bfloat16)
    dims = (((1,), (1,)), ((), ()))
    eh, el = eig_hi[...], eig_lo[...]
    sums = lax.dot_general(high, eh, dims, preferred_element_type=jnp.float32)
    sums += lax.dot_general(high, el, dims, preferred_element_type=jnp.float32)
    sums += lax.dot_general(low, eh, dims, preferred_element_type=jnp.float32)
    for s in range(4):
        for j in range(nsrc):
            part[4 * j + s] = sums[nsrc * s + j : nsrc * s + j + 1, :]

    share = own.shape[0]

    def reduce_copy(off):
        dst = lax.rem(z_me + off, planes)
        return pltpu.make_async_remote_copy(
            src_ref=part.at[pl.ds(dst * share, share)],
            dst_ref=red.at[off - 1],
            send_sem=red_ssem.at[off - 1],
            recv_sem=red_rsem.at[off - 1],
            device_id={"space": dst},
            device_id_type=MESH,
        )

    def gather_copy(off):
        return pltpu.make_async_remote_copy(
            src_ref=own,
            dst_ref=gat.at[off - 1],
            send_sem=gat_ssem.at[off - 1],
            recv_sem=gat_rsem.at[off - 1],
            device_id={"tm": lax.rem(t_me + off, times)},
            device_id_type=MESH,
        )

    for off in range(1, planes):
        reduce_copy(off).start()
    total = part[pl.ds(z_me * share, share)]
    for off in range(1, planes):
        reduce_copy(off).wait_recv()
        total = total + red[off - 1]
    own[...] = total
    for off in range(1, times):
        gather_copy(off).start()
    per_out[...] = total
    weighted = jnp.dot(
        total.reshape(share, 2 * nev),
        onehot[...],
        preferred_element_type=jnp.float32,
        precision=lax.Precision.HIGHEST,
    ).reshape(share, 1, 2 * nev)
    slot = lax.broadcasted_iota(jnp.int32, (share, 1, times), 2)
    value = jnp.sum(weighted * total, axis=-1, keepdims=True)
    result = jnp.where(slot == t_me, value, 0.0)
    for off in range(1, times):
        gather_copy(off).wait_recv()
        value = jnp.sum(weighted * gat[off - 1], axis=-1, keepdims=True)
        result = jnp.where(slot == lax.rem(t_me + times - off, times), value, result)
    cor_out[...] = result
    for off in range(1, planes):
        reduce_copy(off).wait_send()
    for off in range(1, times):
        gather_copy(off).wait_send()


def shards(times, planes, *args):
    noise, gauge, clover, eigvecs = args[:4]
    assert noise.shape[1] == noise.shape[2] == 1
    nsrc, sites, nev = noise.shape[0], noise.shape[-1], eigvecs.shape[0]
    rows = 4 * nsrc
    share = rows // planes
    depth = 6 * sites
    f32 = jnp.float32
    vmem = pl.BlockSpec(memory_space=pltpu.VMEM)
    smem = pl.BlockSpec(memory_space=pltpu.SMEM)
    dma = pltpu.SemaphoreType.DMA
    return pl.pallas_call(
        functools.partial(kernel, times, planes),
        out_shape=(
            jax.ShapeDtypeStruct((share, 1, 2 * nev), f32),
            jax.ShapeDtypeStruct((share, 1, times), f32),
        ),
        in_specs=[vmem] * 4 + [smem] * 3,
        out_specs=(vmem, vmem),
        scratch_shapes=[
            pltpu.VMEM((4, 2, 3, 3, nsrc, sites), f32),
            pltpu.VMEM((2, 2, 6, 6, nsrc, sites), f32),
            pltpu.VMEM((2, 4, 3, nsrc, sites), f32),
            pltpu.VMEM((2, 4, 3, nsrc, sites), f32),
            pltpu.VMEM((2, 4, 3, nsrc, sites), f32),
            pltpu.VMEM((ITERS, 4, 2, 2, 3, nsrc, sites), f32),
            pltpu.VMEM((ITERS, 4, 2, 2, 3, nsrc, sites), f32),
            pltpu.VMEM((2 * nev, depth), jnp.bfloat16),
            pltpu.VMEM((2 * nev, depth), jnp.bfloat16),
            pltpu.VMEM((rows, 1, 2 * nev), f32),
            pltpu.VMEM((planes - 1, share, 1, 2 * nev), f32),
            pltpu.VMEM((share, 1, 2 * nev), f32),
            pltpu.VMEM((times - 1, share, 1, 2 * nev), f32),
            pltpu.VMEM((2 * nev, 2 * nev), f32),
            dma((ITERS, 4)),
            dma((ITERS, 4)),
            dma((planes - 1,)),
            dma((planes - 1,)),
            dma((times - 1,)),
            dma((times - 1,)),
        ],
        compiler_params=pltpu.CompilerParams(
            collective_id=0, has_side_effects=True, vmem_limit_bytes=32 * 1024 * 1024
        ),
    )(*args)


def solution(mesh):
    return jax.shard_map(
        functools.partial(shards, mesh.shape["tm"], mesh.shape["space"]),
        mesh=mesh,
        in_specs=(
            P(None, "tm", "space", None, None),
            P(None, None, "tm", "space", None, None),
            P(None, None, "tm", "space", None, None),
            P(None, "tm", "space", None, None),
            P(),
            P(),
            P(),
        ),
        out_specs=(P("space", "tm", None), P("space", "tm", None)),
        check_vma=False,
    )
```

```python
import functools
import math

import jax
import jax.numpy as jnp
from jax import lax
from jax.experimental import pallas as pl
from jax.experimental.pallas import tpu as pltpu
from jax.sharding import PartitionSpec as P

ITERS = 4
DILUTE = 4
GROUPS = 2
MESH = pl.DeviceIdType.MESH

diag_term = 4.1
step_size = 0.2
twist_table = (
    (((1, 0, -1), (0, 0, -1)), ((1, 0, 1), (0, 0, 1))),
    (((1, -1, 0), (0, 1, 0)), ((1, 1, 0), (0, -1, 0))),
    (((0, 0, -1), (1, 0, 1)), ((0, 0, 1), (1, 0, -1))),
    (((0, 1, 0), (1, 1, 0)), ((0, 1, 0), (1, 1, 0))),
)


def signed_add(total, sign, value):
    return total + value if sign > 0 else total - value


def twist_terms(real_coef, imag_coef, real, imag):
    if imag_coef == 0:
        return (real_coef, real), (real_coef, imag)
    return (-imag_coef, imag), (imag_coef, real)


def kernel(
    times, planes, noise_in, gauge_in, clover_in, eig_in, partner_in, dilution_in, boundary_in,
    per_out, cor_out,
    noise, gauge, clover, eigvecs, partner, dilution, boundary,
    links, clov, src, sol, acc, first_out, first_in, sbuf, rbuf, eig_hi, eig_lo,
    part, red, own, gat, onehot,
    load_sem, first_ssem, first_rsem, ssem, rsem, red_ssem, red_rsem, gat_ssem, gat_rsem,
):
    loads = []
    pairs = (
        (boundary_in, boundary), (dilution_in, dilution), (noise_in, noise), (gauge_in, gauge),
        (clover_in, clover), (eig_in, eigvecs), (partner_in, partner),
    )
    for k, (origin, target) in enumerate(pairs):
        loads.append(pltpu.make_async_copy(origin, target, load_sem.at[k]))
        loads[k].start()

    t_me = lax.axis_index("tm")
    z_me = lax.axis_index("space")
    t_up, t_down = lax.rem(t_me + 1, times), lax.rem(t_me + times - 1, times)
    z_up, z_down = lax.rem(z_me + 1, planes), lax.rem(z_me + planes - 1, planes)

    barrier = pltpu.get_barrier_semaphore()
    for off in range(1, times):
        pl.semaphore_signal(
            barrier, inc=1, device_id={"tm": lax.rem(t_me + off, times)}, device_id_type=MESH
        )
    for off in range(1, planes):
        pl.semaphore_signal(
            barrier, inc=1, device_id={"space": lax.rem(z_me + off, planes)}, device_id_type=MESH
        )

    nsrc, sites = noise.shape[0], noise.shape[-1]
    group, width = nsrc // GROUPS, sites // GROUPS
    side = math.isqrt(sites)
    nev = eigvecs.shape[0]
    row = (1, sites)
    lane = lax.broadcasted_iota(jnp.int32, row, 1)
    x_row, y_row = lax.rem(lane, side), lax.div(lane, side)
    field = (nsrc, width)
    field_row = lax.broadcasted_iota(jnp.int32, field, 0)
    lower = field_row < group

    def spread(value):
        shape = value.shape[:-2] + field
        first = jnp.broadcast_to(value[..., :width], shape)
        second = jnp.broadcast_to(value[..., width:], shape)
        return jnp.where(jnp.broadcast_to(lower, shape), first, second)

    for k in range(4):
        loads[k].wait()
    phases = [1.0 - 2.0 * boundary[mu].astype(jnp.float32) for mu in range(4)]
    half_step = 0.5 * step_size
    one = jnp.ones(row, jnp.float32)
    signs = (
        jnp.where(x_row == side - 1, phases[0], one) * half_step,
        jnp.where(y_row == side - 1, phases[1], one) * half_step,
        jnp.where(z_me == planes - 1, phases[2], 1.0) * half_step * one,
        jnp.where(t_me == times - 1, phases[3], 1.0) * half_step * one,
    )

    def set_links(mu):
        for col in range(3):
            for p in range(2):
                value = gauge[mu, :, 2 * col + p] * signs[mu][None]
                links[mu, p, :, col] = spread(value)

    t_mod = lax.rem(t_me, DILUTE)
    spin_rows = []
    for g in range(GROUPS):
        source_row = lax.rem(field_row, group) + g * group
        spin_rows.append(lax.rem(source_row, 4))
        weight = jnp.zeros(field, jnp.float32)
        for j in range(g * group, (g + 1) * group):
            chosen = jnp.where(dilution[j] == t_mod, step_size, 0.0)
            weight = jnp.where(source_row == j, chosen, weight)
        for color in range(3):
            for p in range(2):
                k = 2 * color + p
                rows = []
                for y_half in range(GROUPS):
                    for j in range(g * group, (g + 1) * group):
                        rows.append(noise[j, k, :, y_half * width : (y_half + 1) * width])
                value = jnp.concatenate(rows, 0) * weight
                for d in (0, 2):
                    first_out[g, d, p, color] = value

    def expand(g, value):
        return jnp.stack([jnp.where(spin_rows[g] == s, value, 0.0) for s in range(4)])

    def half(mu, sign, re, im):
        real, imag = [], []
        for h in range(2):
            pick, rc, ic = twist_table[mu][0][h]
            tr, ti = twist_terms(rc, ic, re[2 + pick], im[2 + pick])
            real.append(signed_add(re[h], sign * tr[0], tr[1]))
            imag.append(signed_add(im[h], sign * ti[0], ti[1]))
        return jnp.stack(real), jnp.stack(imag)

    def forward(mu, vr, vi):
        real = imag = None
        for c in range(3):
            ur, ui = links[mu, 0, :, c][None], links[mu, 1, :, c][None]
            ar, ai = vr[:, c : c + 1], vi[:, c : c + 1]
            dr, di = ur * ar - ui * ai, ur * ai + ui * ar
            real, imag = (dr, di) if c == 0 else (real + dr, imag + di)
        return real, imag

    def adjoint(mu, vr, vi):
        real = imag = None
        for c in range(3):
            ur, ui = links[mu, 0, c][None], links[mu, 1, c][None]
            ar, ai = vr[:, c : c + 1], vi[:, c : c + 1]
            dr, di = ur * ar + ui * ai, ur * ai - ui * ar
            real, imag = (dr, di) if c == 0 else (real + dr, imag + di)
        return real, imag

    def gather_in(g, mu, ahead, behind):
        diff = (behind[0] - ahead[0], behind[1] - ahead[1])
        for p in range(2):
            acc[g, p, 0:2] += ahead[p] + behind[p]
        for h in range(2):
            pick, rc, ic = twist_table[mu][1][h]
            terms = twist_terms(rc, ic, diff[0][pick], diff[1][pick])
            for p in range(2):
                acc[g, p, 2 + h] = signed_add(acc[g, p, 2 + h], terms[p][0], terms[p][1])

    flat = (6 * nsrc, width)
    flat_lane = lax.broadcasted_iota(jnp.int32, flat, 1)
    flat_x = lax.rem(flat_lane, side)
    edge = (6, nsrc, width)
    edge_lane = lax.broadcasted_iota(jnp.int32, edge, 2)

    def shift(mu, ahead, value):
        value = value.reshape(flat)
        if mu == 0:
            if ahead:
                moved = jnp.where(
                    flat_x == side - 1,
                    pltpu.roll(value, side - 1, 1),
                    pltpu.roll(value, width - 1, 1),
                )
            else:
                moved = jnp.where(
                    flat_x == 0,
                    pltpu.roll(value, width - side + 1, 1),
                    pltpu.roll(value, 1, 1),
                )
        else:
            moved = pltpu.roll(value, width - side if ahead else side, 1).reshape(edge)
            other = jnp.concatenate([moved[:, group:], moved[:, :group]], 1)
            moved = jnp.where(
                edge_lane >= width - side if ahead else edge_lane < side, other, moved
            )
        return moved.reshape(2, 3, nsrc, width)

    targets = ({"tm": t_down}, {"tm": t_up}, {"space": z_down}, {"space": z_up})

    def first_copy(g, d):
        return pltpu.make_async_remote_copy(
            src_ref=first_out.at[g, d],
            dst_ref=first_in.at[g, d],
            send_sem=first_ssem.at[g, d],
            recv_sem=first_rsem.at[g, d],
            device_id=targets[d],
            device_id_type=MESH,
        )

    def copy(g, it, d):
        return pltpu.make_async_remote_copy(
            src_ref=sbuf.at[g, it, d],
            dst_ref=rbuf.at[g, it, d],
            send_sem=ssem.at[g, it, d],
            recv_sem=rsem.at[g, it, d],
            device_id=targets[d],
            device_id_type=MESH,
        )

    def send(g, it):
        re, im = sol[g, 0], sol[g, 1]
        for mu, d in ((3, 0), (2, 2)):
            sbuf[g, it, d, 0], sbuf[g, it, d, 1] = half(mu, -1, re, im)
            copy(g, it, d).start()
            behind = adjoint(mu, *half(mu, 1, re, im))
            sbuf[g, it, d + 1, 0], sbuf[g, it, d + 1, 1] = behind
            copy(g, it, d + 1).start()

    def local(g):
        keep = 1.0 - step_size * diag_term
        for h in range(2):
            real = imag = None
            for b in range(6):
                cr, ci = clov[h, 0, :, b], clov[h, 1, :, b]
                vr = sol[g, 0, 2 * h + b // 3, b % 3][None]
                vi = sol[g, 1, 2 * h + b // 3, b % 3][None]
                dr, di = cr * vr - ci * vi, cr * vi + ci * vr
                real, imag = (dr, di) if b == 0 else (real + dr, imag + di)
            for p, value in enumerate((real, imag)):
                lo = 2 * h
                acc[g, p, lo : lo + 2] = (
                    value.reshape(2, 3, nsrc, width)
                    + keep * sol[g, p, lo : lo + 2]
                    + src[g, p, lo : lo + 2]
                )
        re, im = sol[g, 0], sol[g, 1]
        for mu in range(2):
            ahead = half(mu, -1, re, im)
            ahead = forward(mu, shift(mu, True, ahead[0]), shift(mu, True, ahead[1]))
            behind = adjoint(mu, *half(mu, 1, re, im))
            behind = (shift(mu, False, behind[0]), shift(mu, False, behind[1]))
            gather_in(g, mu, ahead, behind)

    def finish(g, it):
        for mu, d in ((2, 2), (3, 0)):
            copy(g, it, d).wait_recv()
            copy(g, it, d + 1).wait_recv()
            ahead = forward(mu, rbuf[g, it, d, 0], rbuf[g, it, d, 1])
            gather_in(g, mu, ahead, (rbuf[g, it, d + 1, 0], rbuf[g, it, d + 1, 1]))
        sol[g] = acc[g]

    def finish_first(g):
        for mu, d in ((2, 2), (3, 0)):
            first_copy(g, d).wait_recv()
            first_copy(g, d + 1).wait_recv()
            ahead = [expand(g, first_in[g, d, p]) for p in range(2)]
            ahead = forward(mu, *half(mu, -1, *ahead))
            behind = [expand(g, first_in[g, d + 1, p]) for p in range(2)]
            gather_in(g, mu, ahead, half(mu, 1, *behind))
        sol[g] = acc[g]

    for mu, d in ((3, 0), (2, 2)):
        set_links(mu)
        for g in range(GROUPS):
            pair = [first_out[g, d, p][None] for p in range(2)]
            re, im = adjoint(mu, *pair)
            first_out[g, d + 1, 0], first_out[g, d + 1, 1] = re[0], im[0]
        if mu == 3:
            pl.semaphore_wait(barrier, times + planes - 2)
        for g in range(GROUPS):
            first_copy(g, d).start()
            first_copy(g, d + 1).start()

    for g in range(GROUPS):
        for p in range(2):
            value = expand(g, first_out[g, 0, p])
            src[g, p] = value
            sol[g, p] = value
    set_links(0)
    set_links(1)
    loads[4].wait()
    for b in range(6):
        for p in range(2):
            clov[:, p, :, b] = spread(clover[:, :, 2 * b + p] * (-step_size))

    for g in range(GROUPS):
        local(g)
    for g in range(GROUPS):
        finish_first(g)
        send(g, 0)
        local(g)

    loads[5].wait()
    for color in range(3):
        real = eigvecs[:, 2 * color].reshape(nev, sites)
        imag = eigvecs[:, 2 * color + 1].reshape(nev, sites)
        for p, (top, bottom) in enumerate(((real, -imag), (imag, real))):
            lo = (2 * color + p) * sites
            whole = jnp.concatenate([top, bottom], 0)
            high = whole.astype(jnp.bfloat16)
            eig_hi[:, lo : lo + sites] = high
            eig_lo[:, lo : lo + sites] = (whole - high.astype(jnp.float32)).astype(jnp.bfloat16)
    loads[6].wait()
    out_lane = lax.broadcasted_iota(jnp.int32, (1, onehot.shape[1]), 1)
    for k in range(nev):
        for p in range(2):
            onehot[p * nev + k : p * nev + k + 1, :] = jnp.where(
                out_lane == partner[k] + p * nev, 1.0, 0.0
            )

    def iteration(it, carry):
        for g in range(GROUPS):
            finish(g, it)
            send(g, it + 1)
            local(g)
        return carry

    lax.fori_loop(0, ITERS - 2, iteration, 0)

    dims = (((1,), (1,)), ((), ()))
    for g in range(GROUPS):
        finish(g, ITERS - 2)
        pieces = []
        for color in range(3):
            for p in range(2):
                for y_half in range(GROUPS):
                    lo = y_half * group
                    rows = [sol[g, p, s, color, lo : lo + group, :] for s in range(4)]
                    pieces.append(jnp.concatenate(rows, 0))
        whole = jnp.concatenate(pieces, 1)
        high = whole.astype(jnp.bfloat16)
        low = (whole - high.astype(jnp.float32)).astype(jnp.bfloat16)
        eh, el = eig_hi[...], eig_lo[...]
        sums = lax.dot_general(high, eh, dims, preferred_element_type=jnp.float32)
        sums += lax.dot_general(high, el, dims, preferred_element_type=jnp.float32)
        sums += lax.dot_general(low, eh, dims, preferred_element_type=jnp.float32)
        for s in range(4):
            for j in range(group):
                k = group * s + j
                part[4 * (g * group + j) + s] = sums[k : k + 1, :]

    share = own.shape[0]

    def reduce_copy(off):
        dst = lax.rem(z_me + off, planes)
        return pltpu.make_async_remote_copy(
            src_ref=part.at[pl.ds(dst * share, share)],
            dst_ref=red.at[off - 1],
            send_sem=red_ssem.at[off - 1],
            recv_sem=red_rsem.at[off - 1],
            device_id={"space": dst},
            device_id_type=MESH,
        )

    def gather_copy(off):
        return pltpu.make_async_remote_copy(
            src_ref=own,
            dst_ref=gat.at[off - 1],
            send_sem=gat_ssem.at[off - 1],
            recv_sem=gat_rsem.at[off - 1],
            device_id={"tm": lax.rem(t_me + off, times)},
            device_id_type=MESH,
        )

    for off in range(1, planes):
        reduce_copy(off).start()
    total = part[pl.ds(z_me * share, share)]
    for off in range(1, planes):
        reduce_copy(off).wait_recv()
        total = total + red[off - 1]
    own[...] = total
    for off in range(1, times):
        gather_copy(off).start()
    per_out[...] = total
    weighted = jnp.dot(
        total.reshape(share, 2 * nev),
        onehot[...],
        preferred_element_type=jnp.float32,
        precision=lax.Precision.HIGHEST,
    ).reshape(share, 1, 2 * nev)
    slot = lax.broadcasted_iota(jnp.int32, (share, 1, times), 2)
    value = jnp.sum(weighted * total, axis=-1, keepdims=True)
    result = jnp.where(slot == t_me, value, 0.0)
    for off in range(1, times):
        gather_copy(off).wait_recv()
        value = jnp.sum(weighted * gat[off - 1], axis=-1, keepdims=True)
        result = jnp.where(slot == lax.rem(t_me + times - off, times), value, result)
    cor_out[...] = result
    for off in range(1, planes):
        reduce_copy(off).wait_send()
    for off in range(1, times):
        gather_copy(off).wait_send()
    for g in range(GROUPS):
        for d in range(4):
            first_copy(g, d).wait_send()
            for it in range(ITERS - 1):
                copy(g, it, d).wait_send()


def shards(times, planes, *args):
    noise, gauge, clover, eigvecs = args[:4]
    assert noise.shape[1] == noise.shape[2] == 1
    nsrc, sites, nev = noise.shape[0], noise.shape[-1], eigvecs.shape[0]
    rows = 4 * nsrc
    share = rows // planes
    depth = 6 * sites
    f32 = jnp.float32
    field = (nsrc, sites // GROUPS)
    args = (
        noise.reshape(nsrc, 6, 1, sites),
        gauge.reshape(4, 3, 6, 1, sites),
        clover.reshape(2, 6, 12, 1, sites),
        eigvecs.reshape(nev, 6, 1, sites),
    ) + args[4:]
    vmem = pl.BlockSpec(memory_space=pltpu.VMEM)
    dma = pltpu.SemaphoreType.DMA
    return pl.pallas_call(
        functools.partial(kernel, times, planes),
        out_shape=(
            jax.ShapeDtypeStruct((share, 1, 2 * nev), f32),
            jax.ShapeDtypeStruct((share, 1, times), f32),
        ),
        in_specs=[pl.BlockSpec(memory_space=pltpu.HBM)] * 7,
        out_specs=(vmem, vmem),
        scratch_shapes=[
            *[pltpu.VMEM(array.shape, f32) for array in args[:4]],
            *[pltpu.SMEM(array.shape, jnp.int32) for array in args[4:]],
            pltpu.VMEM((4, 2, 3, 3) + field, f32),
            pltpu.VMEM((2, 2, 6, 6) + field, f32),
            pltpu.VMEM((GROUPS, 2, 4, 3) + field, f32),
            pltpu.VMEM((GROUPS, 2, 4, 3) + field, f32),
            pltpu.VMEM((GROUPS, 2, 4, 3) + field, f32),
            pltpu.VMEM((GROUPS, 4, 2, 3) + field, f32),
            pltpu.VMEM((GROUPS, 4, 2, 3) + field, f32),
            pltpu.VMEM((GROUPS, ITERS - 1, 4, 2, 2, 3) + field, f32),
            pltpu.VMEM((GROUPS, ITERS - 1, 4, 2, 2, 3) + field, f32),
            pltpu.VMEM((2 * nev, depth), jnp.bfloat16),
            pltpu.VMEM((2 * nev, depth), jnp.bfloat16),
            pltpu.VMEM((rows, 1, 2 * nev), f32),
            pltpu.VMEM((planes - 1, share, 1, 2 * nev), f32),
            pltpu.VMEM((share, 1, 2 * nev), f32),
            pltpu.VMEM((times - 1, share, 1, 2 * nev), f32),
            pltpu.VMEM((2 * nev, 2 * nev), f32),
            dma((len(args),)),
            dma((GROUPS, 4)),
            dma((GROUPS, 4)),
            dma((GROUPS, ITERS - 1, 4)),
            dma((GROUPS, ITERS - 1, 4)),
            dma((planes - 1,)),
            dma((planes - 1,)),
            dma((times - 1,)),
            dma((times - 1,)),
        ],
        compiler_params=pltpu.CompilerParams(
            collective_id=0, has_side_effects=True, vmem_limit_bytes=32 * 1024 * 1024
        ),
    )(*args)


def solution(mesh):
    return jax.shard_map(
        functools.partial(shards, mesh.shape["tm"], mesh.shape["space"]),
        mesh=mesh,
        in_specs=(
            P(None, "tm", "space", None, None),
            P(None, None, "tm", "space", None, None),
            P(None, None, "tm", "space", None, None),
            P(None, "tm", "space", None, None),
            P(),
            P(),
            P(),
        ),
        out_specs=(P("space", "tm", None), P("space", "tm", None)),
        check_vma=False,
    )
```

```python
import functools
import math

import jax
import jax.numpy as jnp
from jax import lax
from jax.experimental import pallas as pl
from jax.experimental.pallas import tpu as pltpu
from jax.sharding import PartitionSpec as P

ITERS = 4
DILUTE = 4
GROUPS = 2
MESH = pl.DeviceIdType.MESH

diag_term = 4.1
step_size = 0.2
twist_table = (
    (((1, 0, -1), (0, 0, -1)), ((1, 0, 1), (0, 0, 1))),
    (((1, -1, 0), (0, 1, 0)), ((1, 1, 0), (0, -1, 0))),
    (((0, 0, -1), (1, 0, 1)), ((0, 0, 1), (1, 0, -1))),
    (((0, 1, 0), (1, 1, 0)), ((0, 1, 0), (1, 1, 0))),
)


def signed_add(total, sign, value):
    return total + value if sign > 0 else total - value


def twist_terms(real_coef, imag_coef, real, imag):
    if imag_coef == 0:
        return (real_coef, real), (real_coef, imag)
    return (-imag_coef, imag), (imag_coef, real)


def kernel(
    times, planes, noise_in, gauge_in, clover_in, eig_in, partner_in, dilution_in, boundary_in,
    per_out, cor_out,
    noise, gauge, clover, eigvecs, partner, dilution, boundary,
    links, clov, src, sol, acc, first_out, first_in, sbuf, rbuf, eig_hi, eig_lo,
    part, red, own, gat, onehot,
    load_sem, first_ssem, first_rsem, ssem, rsem, red_ssem, red_rsem, gat_ssem, gat_rsem,
):
    loads = []
    pairs = (
        (boundary_in, boundary), (dilution_in, dilution), (noise_in, noise), (gauge_in, gauge),
        (clover_in, clover), (eig_in, eigvecs), (partner_in, partner),
    )
    for k, (origin, target) in enumerate(pairs):
        loads.append(pltpu.make_async_copy(origin, target, load_sem.at[k]))
        loads[k].start()

    t_me = lax.axis_index("tm")
    z_me = lax.axis_index("space")
    t_up, t_down = lax.rem(t_me + 1, times), lax.rem(t_me + times - 1, times)
    z_up, z_down = lax.rem(z_me + 1, planes), lax.rem(z_me + planes - 1, planes)

    barrier = pltpu.get_barrier_semaphore()
    for off in range(1, times):
        pl.semaphore_signal(
            barrier, inc=1, device_id={"tm": lax.rem(t_me + off, times)}, device_id_type=MESH
        )
    for off in range(1, planes):
        pl.semaphore_signal(
            barrier, inc=1, device_id={"space": lax.rem(z_me + off, planes)}, device_id_type=MESH
        )

    nsrc, sites = noise.shape[0], noise.shape[-1]
    group, width = nsrc // GROUPS, sites // GROUPS
    side = math.isqrt(sites)
    nev = eigvecs.shape[0]
    row = (1, sites)
    lane = lax.broadcasted_iota(jnp.int32, row, 1)
    x_row, y_row = lax.rem(lane, side), lax.div(lane, side)
    field = (nsrc, width)
    field_row = lax.broadcasted_iota(jnp.int32, field, 0)
    lower = field_row < group

    def spread(value):
        shape = value.shape[:-2] + field
        first = jnp.broadcast_to(value[..., :width], shape)
        second = jnp.broadcast_to(value[..., width:], shape)
        return jnp.where(jnp.broadcast_to(lower, shape), first, second)

    for k in range(4):
        loads[k].wait()
    phases = [1.0 - 2.0 * boundary[mu].astype(jnp.float32) for mu in range(4)]
    half_step = 0.5 * step_size
    one = jnp.ones(row, jnp.float32)
    signs = (
        jnp.where(x_row == side - 1, phases[0], one) * half_step,
        jnp.where(y_row == side - 1, phases[1], one) * half_step,
        jnp.where(z_me == planes - 1, phases[2], 1.0) * half_step * one,
        jnp.where(t_me == times - 1, phases[3], 1.0) * half_step * one,
    )

    def set_links(mu):
        for col in range(3):
            for p in range(2):
                value = gauge[mu, :, 2 * col + p] * signs[mu][None]
                links[mu, p, :, col] = spread(value)

    t_mod = lax.rem(t_me, DILUTE)
    spin_rows = []
    for g in range(GROUPS):
        source_row = lax.rem(field_row, group) + g * group
        spin_rows.append(lax.rem(source_row, 4))
        weight = jnp.zeros(field, jnp.float32)
        for j in range(g * group, (g + 1) * group):
            chosen = jnp.where(dilution[j] == t_mod, step_size, 0.0)
            weight = jnp.where(source_row == j, chosen, weight)
        for color in range(3):
            for p in range(2):
                k = 2 * color + p
                rows = []
                for y_half in range(GROUPS):
                    for j in range(g * group, (g + 1) * group):
                        rows.append(noise[j, k, :, y_half * width : (y_half + 1) * width])
                value = jnp.concatenate(rows, 0) * weight
                for d in (0, 2):
                    first_out[g, d, p, color] = value

    def expand(g, value):
        return jnp.stack([jnp.where(spin_rows[g] == s, value, 0.0) for s in range(4)])

    def half(mu, sign, re, im):
        real, imag = [], []
        for h in range(2):
            pick, rc, ic = twist_table[mu][0][h]
            tr, ti = twist_terms(rc, ic, re[2 + pick], im[2 + pick])
            real.append(signed_add(re[h], sign * tr[0], tr[1]))
            imag.append(signed_add(im[h], sign * ti[0], ti[1]))
        return jnp.stack(real), jnp.stack(imag)

    def forward(mu, vr, vi):
        real = imag = None
        for c in range(3):
            ur, ui = links[mu, 0, :, c][None], links[mu, 1, :, c][None]
            ar, ai = vr[:, c : c + 1], vi[:, c : c + 1]
            dr, di = ur * ar - ui * ai, ur * ai + ui * ar
            real, imag = (dr, di) if c == 0 else (real + dr, imag + di)
        return real, imag

    def adjoint(mu, vr, vi):
        real = imag = None
        for c in range(3):
            ur, ui = links[mu, 0, c][None], links[mu, 1, c][None]
            ar, ai = vr[:, c : c + 1], vi[:, c : c + 1]
            dr, di = ur * ar + ui * ai, ur * ai - ui * ar
            real, imag = (dr, di) if c == 0 else (real + dr, imag + di)
        return real, imag

    def gather_in(g, mu, ahead, behind):
        diff = (behind[0] - ahead[0], behind[1] - ahead[1])
        for p in range(2):
            acc[g, p, 0:2] += ahead[p] + behind[p]
        for h in range(2):
            pick, rc, ic = twist_table[mu][1][h]
            terms = twist_terms(rc, ic, diff[0][pick], diff[1][pick])
            for p in range(2):
                acc[g, p, 2 + h] = signed_add(acc[g, p, 2 + h], terms[p][0], terms[p][1])

    flat = (6 * nsrc, width)
    flat_lane = lax.broadcasted_iota(jnp.int32, flat, 1)
    flat_x = lax.rem(flat_lane, side)
    edge = (6, nsrc, width)
    edge_lane = lax.broadcasted_iota(jnp.int32, edge, 2)

    def shift(mu, ahead, value):
        value = value.reshape(flat)
        if mu == 0:
            if ahead:
                moved = jnp.where(
                    flat_x == side - 1,
                    pltpu.roll(value, side - 1, 1),
                    pltpu.roll(value, width - 1, 1),
                )
            else:
                moved = jnp.where(
                    flat_x == 0,
                    pltpu.roll(value, width - side + 1, 1),
                    pltpu.roll(value, 1, 1),
                )
        else:
            moved = pltpu.roll(value, width - side if ahead else side, 1).reshape(edge)
            other = jnp.concatenate([moved[:, group:], moved[:, :group]], 1)
            moved = jnp.where(
                edge_lane >= width - side if ahead else edge_lane < side, other, moved
            )
        return moved.reshape(2, 3, nsrc, width)

    targets = ({"tm": t_down}, {"tm": t_up}, {"space": z_down}, {"space": z_up})

    def first_copy(g, d):
        return pltpu.make_async_remote_copy(
            src_ref=first_out.at[g, d],
            dst_ref=first_in.at[g, d],
            send_sem=first_ssem.at[g, d],
            recv_sem=first_rsem.at[g, d],
            device_id=targets[d],
            device_id_type=MESH,
        )

    def copy(g, it, d):
        return pltpu.make_async_remote_copy(
            src_ref=sbuf.at[g, it, d],
            dst_ref=rbuf.at[g, it, d],
            send_sem=ssem.at[g, it, d],
            recv_sem=rsem.at[g, it, d],
            device_id=targets[d],
            device_id_type=MESH,
        )

    def send(g, it):
        re, im = sol[g, 0], sol[g, 1]
        for mu, d in ((3, 0), (2, 2)):
            sbuf[g, it, d, 0], sbuf[g, it, d, 1] = half(mu, -1, re, im)
            copy(g, it, d).start()
            behind = adjoint(mu, *half(mu, 1, re, im))
            sbuf[g, it, d + 1, 0], sbuf[g, it, d + 1, 1] = behind
            copy(g, it, d + 1).start()

    def local(g):
        keep = 1.0 - step_size * diag_term
        for h in range(2):
            real = imag = None
            for b in range(6):
                cr, ci = clov[h, 0, :, b], clov[h, 1, :, b]
                vr = sol[g, 0, 2 * h + b // 3, b % 3][None]
                vi = sol[g, 1, 2 * h + b // 3, b % 3][None]
                dr, di = cr * vr - ci * vi, cr * vi + ci * vr
                real, imag = (dr, di) if b == 0 else (real + dr, imag + di)
            for p, value in enumerate((real, imag)):
                lo = 2 * h
                acc[g, p, lo : lo + 2] = (
                    value.reshape(2, 3, nsrc, width)
                    + keep * sol[g, p, lo : lo + 2]
                    + src[g, p, lo : lo + 2]
                )
        re, im = sol[g, 0], sol[g, 1]
        for mu in range(2):
            ahead = half(mu, -1, re, im)
            ahead = forward(mu, shift(mu, True, ahead[0]), shift(mu, True, ahead[1]))
            behind = adjoint(mu, *half(mu, 1, re, im))
            behind = (shift(mu, False, behind[0]), shift(mu, False, behind[1]))
            gather_in(g, mu, ahead, behind)

    def finish(g, it):
        for mu, d in ((2, 2), (3, 0)):
            copy(g, it, d).wait_recv()
            copy(g, it, d + 1).wait_recv()
            ahead = forward(mu, rbuf[g, it, d, 0], rbuf[g, it, d, 1])
            gather_in(g, mu, ahead, (rbuf[g, it, d + 1, 0], rbuf[g, it, d + 1, 1]))
        sol[g] = acc[g]

    def finish_first(g):
        for mu, d in ((2, 2), (3, 0)):
            first_copy(g, d).wait_recv()
            first_copy(g, d + 1).wait_recv()
            ahead = [expand(g, first_in[g, d, p]) for p in range(2)]
            ahead = forward(mu, *half(mu, -1, *ahead))
            behind = [expand(g, first_in[g, d + 1, p]) for p in range(2)]
            gather_in(g, mu, ahead, half(mu, 1, *behind))
        sol[g] = acc[g]

    for mu, d in ((3, 0), (2, 2)):
        set_links(mu)
        for g in range(GROUPS):
            pair = [first_out[g, d, p][None] for p in range(2)]
            re, im = adjoint(mu, *pair)
            first_out[g, d + 1, 0], first_out[g, d + 1, 1] = re[0], im[0]
        if mu == 3:
            pl.semaphore_wait(barrier, times + planes - 2)
        for g in range(GROUPS):
            first_copy(g, d).start()
            first_copy(g, d + 1).start()

    for g in range(GROUPS):
        for p in range(2):
            value = expand(g, first_out[g, 0, p])
            src[g, p] = value
            sol[g, p] = value
    set_links(0)
    set_links(1)
    loads[4].wait()
    for b in range(6):
        for p in range(2):
            clov[:, p, :, b] = spread(clover[:, :, 2 * b + p] * (-step_size))

    for g in range(GROUPS):
        local(g)
    for g in range(GROUPS):
        finish_first(g)
        send(g, 0)
        local(g)

    loads[5].wait()
    for color in range(3):
        real = eigvecs[:, 2 * color].reshape(nev, sites)
        imag = eigvecs[:, 2 * color + 1].reshape(nev, sites)
        for p, (top, bottom) in enumerate(((real, -imag), (imag, real))):
            lo = (2 * color + p) * sites
            whole = jnp.concatenate([top, bottom], 0)
            high = whole.astype(jnp.bfloat16)
            eig_hi[:, lo : lo + sites] = high
            eig_lo[:, lo : lo + sites] = (whole - high.astype(jnp.float32)).astype(jnp.bfloat16)
    loads[6].wait()
    out_lane = lax.broadcasted_iota(jnp.int32, (1, onehot.shape[1]), 1)
    for k in range(nev):
        for p in range(2):
            onehot[p * nev + k : p * nev + k + 1, :] = jnp.where(
                out_lane == partner[k] + p * nev, 1.0, 0.0
            )

    def iteration(it, carry):
        for g in range(GROUPS):
            finish(g, it)
            send(g, it + 1)
            local(g)
        return carry

    lax.fori_loop(0, ITERS - 2, iteration, 0)

    dims = (((1,), (1,)), ((), ()))
    for g in range(GROUPS):
        finish(g, ITERS - 2)
        pieces = []
        for color in range(3):
            for p in range(2):
                for y_half in range(GROUPS):
                    lo = y_half * group
                    rows = [sol[g, p, s, color, lo : lo + group, :] for s in range(4)]
                    pieces.append(jnp.concatenate(rows, 0))
        whole = jnp.concatenate(pieces, 1)
        high = whole.astype(jnp.bfloat16)
        low = (whole - high.astype(jnp.float32)).astype(jnp.bfloat16)
        eh, el = eig_hi[...], eig_lo[...]
        sums = lax.dot_general(high, eh, dims, preferred_element_type=jnp.float32)
        sums += lax.dot_general(high, el, dims, preferred_element_type=jnp.float32)
        sums += lax.dot_general(low, eh, dims, preferred_element_type=jnp.float32)
        for s in range(4):
            for j in range(group):
                k = group * s + j
                part[4 * (g * group + j) + s] = sums[k : k + 1, :]

    share = own.shape[0]

    def reduce_copy(off):
        dst = lax.rem(z_me + off, planes)
        return pltpu.make_async_remote_copy(
            src_ref=part.at[pl.ds(dst * share, share)],
            dst_ref=red.at[off - 1],
            send_sem=red_ssem.at[off - 1],
            recv_sem=red_rsem.at[off - 1],
            device_id={"space": dst},
            device_id_type=MESH,
        )

    def gather_copy(off):
        return pltpu.make_async_remote_copy(
            src_ref=own,
            dst_ref=gat.at[off - 1],
            send_sem=gat_ssem.at[off - 1],
            recv_sem=gat_rsem.at[off - 1],
            device_id={"tm": lax.rem(t_me + off, times)},
            device_id_type=MESH,
        )

    for off in range(1, planes):
        reduce_copy(off).start()
    total = part[pl.ds(z_me * share, share)]
    for off in range(1, planes):
        reduce_copy(off).wait_recv()
        total = total + red[off - 1]
    own[...] = total
    for off in range(1, times):
        gather_copy(off).start()
    per_out[...] = total
    weighted = jnp.dot(
        total.reshape(share, 2 * nev),
        onehot[...],
        preferred_element_type=jnp.float32,
        precision=lax.Precision.HIGHEST,
    ).reshape(share, 1, 2 * nev)
    slot = lax.broadcasted_iota(jnp.int32, (share, 1, times), 2)
    value = jnp.sum(weighted * total, axis=-1, keepdims=True)
    result = jnp.where(slot == t_me, value, 0.0)
    for off in range(1, times):
        gather_copy(off).wait_recv()
        value = jnp.sum(weighted * gat[off - 1], axis=-1, keepdims=True)
        result = jnp.where(slot == lax.rem(t_me + times - off, times), value, result)
    cor_out[...] = result
    for off in range(1, planes):
        reduce_copy(off).wait_send()
    for off in range(1, times):
        gather_copy(off).wait_send()
    for g in range(GROUPS):
        for d in range(4):
            first_copy(g, d).wait_send()
            for it in range(ITERS - 1):
                copy(g, it, d).wait_send()


def shards(times, planes, *args):
    noise, gauge, clover, eigvecs = args[:4]
    assert noise.shape[1] == noise.shape[2] == 1
    nsrc, sites, nev = noise.shape[0], noise.shape[-1], eigvecs.shape[0]
    rows = 4 * nsrc
    share = rows // planes
    depth = 6 * sites
    f32 = jnp.float32
    field = (nsrc, sites // GROUPS)
    args = (
        noise.reshape(nsrc, 6, 1, sites),
        gauge.reshape(4, 3, 6, 1, sites),
        clover.reshape(2, 6, 12, 1, sites),
        eigvecs.reshape(nev, 6, 1, sites),
    ) + args[4:]
    vmem = pl.BlockSpec(memory_space=pltpu.VMEM)
    dma = pltpu.SemaphoreType.DMA
    return pl.pallas_call(
        functools.partial(kernel, times, planes),
        out_shape=(
            jax.ShapeDtypeStruct((share, 1, 2 * nev), f32),
            jax.ShapeDtypeStruct((share, 1, times), f32),
        ),
        in_specs=[pl.BlockSpec(memory_space=pltpu.HBM)] * 7,
        out_specs=(vmem, vmem),
        scratch_shapes=[
            *[pltpu.VMEM(array.shape, f32) for array in args[:4]],
            *[pltpu.SMEM(array.shape, jnp.int32) for array in args[4:]],
            pltpu.VMEM((4, 2, 3, 3) + field, f32),
            pltpu.VMEM((2, 2, 6, 6) + field, f32),
            pltpu.VMEM((GROUPS, 2, 4, 3) + field, f32),
            pltpu.VMEM((GROUPS, 2, 4, 3) + field, f32),
            pltpu.VMEM((GROUPS, 2, 4, 3) + field, f32),
            pltpu.VMEM((GROUPS, 4, 2, 3) + field, f32),
            pltpu.VMEM((GROUPS, 4, 2, 3) + field, f32),
            pltpu.VMEM((GROUPS, ITERS - 1, 4, 2, 2, 3) + field, f32),
            pltpu.VMEM((GROUPS, ITERS - 1, 4, 2, 2, 3) + field, f32),
            pltpu.VMEM((2 * nev, depth), jnp.bfloat16),
            pltpu.VMEM((2 * nev, depth), jnp.bfloat16),
            pltpu.VMEM((rows, 1, 2 * nev), f32),
            pltpu.VMEM((planes - 1, share, 1, 2 * nev), f32),
            pltpu.VMEM((share, 1, 2 * nev), f32),
            pltpu.VMEM((times - 1, share, 1, 2 * nev), f32),
            pltpu.VMEM((2 * nev, 2 * nev), f32),
            dma((len(args),)),
            dma((GROUPS, 4)),
            dma((GROUPS, 4)),
            dma((GROUPS, ITERS - 1, 4)),
            dma((GROUPS, ITERS - 1, 4)),
            dma((planes - 1,)),
            dma((planes - 1,)),
            dma((times - 1,)),
            dma((times - 1,)),
        ],
        compiler_params=pltpu.CompilerParams(
            collective_id=0, has_side_effects=True, vmem_limit_bytes=60 * 1024 * 1024
        ),
    )(*args)


def solution(mesh):
    return jax.shard_map(
        functools.partial(shards, mesh.shape["tm"], mesh.shape["space"]),
        mesh=mesh,
        in_specs=(
            P(None, "tm", "space", None, None),
            P(None, None, "tm", "space", None, None),
            P(None, None, "tm", "space", None, None),
            P(None, "tm", "space", None, None),
            P(),
            P(),
            P(),
        ),
        out_specs=(P("space", "tm", None), P("space", "tm", None)),
        check_vma=False,
    )
```
